32 devices in a mesh: occ: 8 (over z, x), vir: 4 (over y, core).
Axes of the slice: x: 2, y: 2, z: 4, core: 2. Of those that a mesh axis runs over, the one named last changes fastest.
Arguments:
- amps: float32 [1024, 4, 1024], P('occ', 'vir'), may hold values from -6 to 6
- resid: float32 [1024, 4, 1024], P('occ', 'vir'), may hold values from -6 to 6
- ints: float32 [4, 1024, 1024], P('vir', 'occ'), may hold values from -0.5 to 0.5
- tasks: int32 [4], replicated, may hold values from 0 to 3
- pair_tiles: int32 [4, 2], replicated, may hold values from 0 to 18
- irreps: int32 [19, 32], replicated, may hold values from 0 to 7
Outputs:
- updated: float32 [1024, 4, 1024], P('occ', 'vir')
The draws below stay inside these ranges and needn't reach their ends.
All inputs are finite; a program needn't handle non-finite values.
Results may differ from the reference program's by a relative error of at most 0.0003.
Values sent between devices are 32-bit elements; how exact they have to be, the bound alone decides.
No kernel may reach another device: no remote copies, remote signals or barrier semaphores. Data moves between devices by JAX's collectives and lax.ppermute only.
A program may use at most 64 MiB of HBM per device.

```python
import jax
import jax.numpy as jnp
from jax import lax

TILE = 32
NVT = 19
PT = 1024
NPT = 4
O2 = 1024


def touch_ends(result, stream_key, least, top_value):
    dims = result.shape
    spot = [jax.random.randint(jax.random.fold_in(stream_key, axis), (), 0, dims[axis]) for axis in range(len(dims))]
    result = result.at[tuple(spot)].set(least)
    longest = dims.index(max(dims))
    spot[longest] = (spot[longest] + 1) % dims[longest]
    return result.at[tuple(spot)].set(top_value)


def steps_of(stream_key, dims, cuts, smallest, largest):
    factor_of, own = 1.0, jax.random.fold_in(stream_key, 6)
    for position, parts in cuts:
        heights = jnp.exp(jax.random.uniform(jax.random.fold_in(own, position), (parts,), jnp.float32, smallest / len(cuts), largest / len(cuts)))
        factor_of = factor_of * jnp.repeat(heights, dims[position] // parts).reshape([-1 if axis == position else 1 for axis in range(len(dims))])
    return factor_of


def normal_values(rng, extent, spread, bound, cuts=(), kind=jnp.bfloat16):
    loudness = steps_of(rng, extent, cuts, -0.22, 0.18) if cuts else 1.0
    array = jax.random.normal(rng, extent, jnp.float32) * spread * loudness
    return jnp.minimum(jnp.maximum(array, -bound), bound).astype(kind)


def setup_inputs(seed: int = 0) -> dict:
    key_list = jax.random.split(jax.random.key(seed), 7)
    amps = normal_values(key_list[0], (O2, NPT, PT), 1.0, 6.0, ((0, 8), (1, 4)), jnp.float32)
    resid = normal_values(key_list[1], (O2, NPT, PT), 1.0, 6.0, ((0, 8), (1, 4)), jnp.float32)
    ints = normal_values(key_list[2], (NPT, PT, PT), (PT // 8) ** -0.5, 0.5, ((0, 4), (1, 8)), jnp.float32)
    tasks = touch_ends(jax.random.randint(key_list[3], (NPT,), 0, NPT), jax.random.fold_in(key_list[3], 1), 0, NPT - 1).astype(jnp.int32)
    pair_tiles = touch_ends(jax.random.randint(key_list[4], (NPT, 2), 0, NVT), jax.random.fold_in(key_list[4], 1), 0, NVT - 1).astype(jnp.int32)
    irreps = touch_ends(jax.random.randint(key_list[5], (NVT, TILE), 0, 8), jax.random.fold_in(key_list[5], 1), 0, 7).astype(jnp.int32)
    return dict(amps=amps, resid=resid, ints=ints, tasks=tasks, pair_tiles=pair_tiles, irreps=irreps)


def pair_irreps(tile_pair, irreps):
    first_row = irreps[tile_pair[0]]
    second_row = irreps[tile_pair[1]]
    return jnp.bitwise_xor(first_row[:, None], second_row[None, :]).reshape(-1)


def reference(amps, resid, ints, tasks, pair_tiles, irreps):
    def ladder_tile(task_index):
        cd_tile = tasks[task_index]
        selected = lax.dynamic_index_in_dim(amps, cd_tile, 1, keepdims=False)
        ab_irrep = pair_irreps(pair_tiles[task_index], irreps)
        cd_irrep = pair_irreps(pair_tiles[cd_tile], irreps)
        effective = jnp.where(ab_irrep[:, None] == cd_irrep[None, :], ints[task_index], jnp.zeros((), ints.dtype))
        return lax.dot_general(selected, effective, (((1,), (1,)), ((), ())), precision=lax.Precision.HIGHEST, preferred_element_type=jnp.float32)
    ladder = lax.map(ladder_tile, jnp.arange(NPT, dtype=jnp.int32))
    return resid + jnp.transpose(ladder, (1, 0, 2))
```

```python
import functools

import jax
import jax.numpy as jnp
from jax import lax
from jax.experimental import pallas as pl
from jax.experimental.pallas import tpu as pltpu
from jax.sharding import PartitionSpec as P

GROUP = 8
LANES = 128
DEPTH = 192

NT = (((1,), (1,)), ((), ()))
NN = (((1,), (0,)), ((), ()))


def dot(left, right, dims):
    return lax.dot_general(left, right, dims, preferred_element_type=jnp.float32)


def split(values):
    high = values.astype(jnp.bfloat16)
    return high, (values - high.astype(jnp.float32)).astype(jnp.bfloat16)


def iota(shape, dim):
    return lax.broadcasted_iota(jnp.int32, shape, dim)


def pair_rows(firsts, seconds, width):
    tile = firsts.shape[1]
    column, orbital = iota((tile, width), 1), iota((tile, width), 0)
    outer = (lax.div(column, tile) == orbital).astype(jnp.bfloat16)
    inner = (lax.rem(column, tile) == orbital).astype(jnp.bfloat16)
    spread = lambda rows, how: dot(rows.astype(jnp.float32).astype(jnp.bfloat16), how, NN).astype(jnp.int32)
    return jnp.bitwise_xor(spread(firsts, outer), spread(seconds, inner))


def ranks(irrep):
    width = irrep.shape[1]
    member = (irrep == iota(irrep.shape, 0)).astype(jnp.float32)
    parts = [member[:, at : at + LANES] for at in range(0, width, LANES)]
    before = (iota((LANES, LANES), 0) < iota((LANES, LANES), 1)).astype(jnp.bfloat16)
    inside = dot(jnp.concatenate(parts, axis=0).astype(jnp.bfloat16), before, NN)
    base = jnp.zeros((GROUP, 1), jnp.float32)
    out = []
    for place, part in enumerate(parts):
        count = inside[place * GROUP : (place + 1) * GROUP] + base
        out.append(jnp.sum(part * count, axis=0, keepdims=True))
        base = base + jnp.sum(part, axis=1, keepdims=True)
    return jnp.concatenate(out, axis=1).astype(jnp.int32)


def prep_kernel(depth, first_ref, tasks_ref, pairs_ref, irreps_ref, ints_ref, buf_ref, meta_ref):
    own, block = lax.axis_index("vir"), lax.axis_index("occ")
    height, width = ints_ref.shape
    tile = irreps_ref.shape[1]
    first = first_ref[0]
    cd = tasks_ref[own]
    row = lambda pair, side: irreps_ref[pl.ds(pairs_ref[pair, side], 1), :]
    wide = lambda values: jnp.broadcast_to(values, (GROUP, tile))
    ab_outer, ab_inner = row(own, 0), row(own, 1)
    irrep = pair_rows(
        jnp.concatenate([wide(row(cd, 0)), wide(ab_outer)], axis=0),
        jnp.concatenate([wide(row(cd, 1)), wide(ab_inner)], axis=0),
        width,
    )
    cd_irrep, ab_irrep = irrep[:GROUP], irrep[GROUP:]
    rank = ranks(cd_irrep) - first
    inside = jnp.logical_and(rank >= 0, rank < depth)
    slot = jnp.where(inside, cd_irrep[:1] * depth + rank, -1)
    meta_ref[...] = jnp.where(iota((GROUP, width), 0) == 0, jnp.broadcast_to(slot, (GROUP, width)), ab_irrep)
    pair = iota((height, tile), 0) + block * height
    lane = iota((height, tile), 1)
    outer = jnp.sum(jnp.where(lane == lax.div(pair, tile), ab_outer, 0), axis=1, keepdims=True)
    inner = jnp.sum(jnp.where(lane == lax.rem(pair, tile), ab_inner, 0), axis=1, keepdims=True)
    live = jnp.bitwise_xor(outer, inner) == cd_irrep[:1]
    high, low = split(jnp.where(live, ints_ref[...], 0.0))
    pick = (iota((depth, width), 0) == rank).astype(jnp.bfloat16)
    buf_ref[...] = dot(pick, high, NT) + dot(pick, low, NT)


def prep(first, tasks, pairs, irreps, ints, depth):
    height, width = ints.shape
    smem, vmem = pl.BlockSpec(memory_space=pltpu.SMEM), pl.BlockSpec(memory_space=pltpu.VMEM)
    return pl.pallas_call(
        functools.partial(prep_kernel, depth),
        out_shape=(
            jax.ShapeDtypeStruct((depth, height), jnp.float32),
            jax.ShapeDtypeStruct((GROUP, width), jnp.int32),
        ),
        in_specs=[smem, smem, smem, vmem, vmem],
        out_specs=(vmem, vmem),
        compiler_params=pltpu.CompilerParams(vmem_limit_bytes=32 << 20),
        cost_estimate=pl.CostEstimate(flops=4 * depth * height * width, bytes_accessed=4 * height * width, transcendentals=0),
        name="compact",
    )(first, tasks, pairs, irreps, ints)


def order_kernel(depth, count, *refs):
    tasks_ref, pairs_ref, irreps_ref, meta_ref = refs[:4]
    tiles, (out_ref, most_ref, held, sem) = refs[4 : 4 + count], refs[4 + count :]
    own = lax.axis_index("vir")
    chosen = jnp.bitwise_xor(tasks_ref[own], own)
    for number, tile_ref in enumerate(tiles):

        @pl.when(chosen == number)
        def _(tile_ref=tile_ref):
            copy = pltpu.make_async_copy(tile_ref.at[:, 0, :], held, sem)
            copy.start()
            copy.wait()

    width = meta_ref.shape[1]
    rows = lambda side: jnp.concatenate(
        [irreps_ref[pl.ds(pairs_ref[tasks_ref[k], side], 1), :] for k in range(tasks_ref.shape[0])], axis=0
    )
    irrep = pair_rows(rows(0), rows(1), width)
    most = jnp.zeros((irrep.shape[0], 1), jnp.int32)
    for g in range(GROUP):
        most = jnp.maximum(most, jnp.sum((irrep == g).astype(jnp.int32), axis=1, keepdims=True))
    most_ref[0] = jnp.max(most)

    high, low = split(held[...])
    both = jnp.concatenate([high, low], axis=0)
    for at in range(0, GROUP * depth, GROUP * depth // 4):
        size = GROUP * depth // 4
        place = (iota((size, width), 0) + at == meta_ref[:1]).astype(jnp.bfloat16)
        out_ref[:, at : at + size] = dot(both, place, NT).astype(jnp.bfloat16)


def order(tasks, pairs, irreps, meta, tiles, depth):
    height, _, width = tiles[0].shape
    smem, vmem = pl.BlockSpec(memory_space=pltpu.SMEM), pl.BlockSpec(memory_space=pltpu.VMEM)
    return pl.pallas_call(
        functools.partial(order_kernel, depth, len(tiles)),
        out_shape=(
            jax.ShapeDtypeStruct((2 * height, GROUP * depth), jnp.bfloat16),
            jax.ShapeDtypeStruct((1,), jnp.int32),
        ),
        in_specs=[smem, smem, vmem, vmem] + [pl.BlockSpec(memory_space=pl.ANY)] * len(tiles),
        out_specs=(vmem, smem),
        scratch_shapes=[pltpu.VMEM((height, width), jnp.float32), pltpu.SemaphoreType.DMA],
        compiler_params=pltpu.CompilerParams(vmem_limit_bytes=32 << 20),
        cost_estimate=pl.CostEstimate(
            flops=4 * height * width * GROUP * depth, bytes_accessed=4 * height * width, transcendentals=0
        ),
        name="order_amplitudes",
    )(tasks, pairs, irreps, meta, *tiles)


def ladder_kernel(depth, masks, meta_ref, amps_ref, *refs):
    count = len(masks)
    pieces, (base_ref, out_ref, held, sems) = refs[:count], refs[count:]
    block = lax.axis_index("occ")
    height = held.shape[0]
    size = pieces[0].shape[1]
    places = [pl.ds(pl.multiple_of(jnp.bitwise_xor(block, mask) * size, LANES), size) for mask in masks]
    loads = [
        pltpu.make_async_copy(base_ref.at[:, 0, place], held.at[:, n * size : (n + 1) * size], sems.at[n])
        for n, place in enumerate(places)
    ]
    for load in loads:
        load.start()
    high, low = split(jnp.concatenate([piece[...] for piece in pieces], axis=1))
    irrep = jnp.concatenate([meta_ref[1:2, place] for place in places], axis=1)
    zero = jnp.zeros((), jnp.bfloat16)
    blocks = lambda values: jnp.concatenate([jnp.where(irrep == g, values, zero) for g in range(GROUP)], axis=0)
    both = dot(amps_ref[...], blocks(high), NN)
    ladder = both[:height] + both[height:] + dot(amps_ref[:height], blocks(low), NN)
    for load in loads:
        load.wait()
    held[...] += ladder
    stores = [
        pltpu.make_async_copy(held.at[:, n * size : (n + 1) * size], out_ref.at[:, 0, place], sems.at[n])
        for n, place in enumerate(places)
    ]
    for store in stores:
        store.start()
    for store in stores:
        store.wait()


def ladder(meta, amps, masks, pieces, base, depth):
    height, size = base.shape[0], pieces[0].shape[1]
    vmem, hbm = pl.BlockSpec(memory_space=pltpu.VMEM), pl.BlockSpec(memory_space=pl.ANY)
    columns = size * len(pieces)
    return pl.pallas_call(
        functools.partial(ladder_kernel, depth, masks),
        out_shape=jax.ShapeDtypeStruct(base.shape, base.dtype),
        in_specs=[vmem, vmem] + [vmem] * len(pieces) + [hbm],
        out_specs=hbm,
        scratch_shapes=[pltpu.VMEM((height, columns), jnp.float32), pltpu.SemaphoreType.DMA((len(pieces),))],
        input_output_aliases={2 + len(pieces): 0},
        compiler_params=pltpu.CompilerParams(vmem_limit_bytes=48 << 20),
        cost_estimate=pl.CostEstimate(
            flops=6 * height * columns * GROUP * depth, bytes_accessed=8 * height * columns, transcendentals=0
        ),
        name="ladder",
    )(meta, amps, *pieces, base)


def swap(values, axis, size, mask):
    return lax.ppermute(values, axis, [(device, device ^ mask) for device in range(size)])


def spread_tiles(amps, size):
    tiles = {0: amps}
    bit = size >> 1
    while bit:
        for number in sorted(tiles):
            tiles[number | bit] = swap(tiles[number], "vir", size, bit)
        bit >>= 1
    return [tiles[number] for number in range(size)]


def shards(occ_size, vir_size, amps, resid, ints, tasks, pair_tiles, irreps):
    rows = ints[0]
    height, width = rows.shape
    depth = min(DEPTH, width)

    def exchange(buf):
        if height % LANES:
            return [((0,), [lax.all_gather(buf, "occ", axis=1, tiled=True)])]
        near = {0: buf}
        for mask in range(2, occ_size, 2):
            near[mask] = swap(buf, "occ", occ_size, mask)
        far = {mask | 1: swap(piece, "occ", occ_size, 1) for mask, piece in near.items()} if occ_size > 1 else {}
        return [(tuple(part), list(part.values())) for part in (near, far) if part]

    def add_round(first, base, tiles):
        buf, meta = prep(first, tasks, pair_tiles, irreps, rows, depth)
        groups = exchange(buf)
        ordered, most = order(tasks, pair_tiles, irreps, meta, tiles, depth)
        for masks, pieces in groups:
            base = ladder(meta, ordered, masks, pieces, base, depth)
        return base, most

    tiles = spread_tiles(amps, vir_size)
    out, most = add_round(jnp.zeros((1,), jnp.int32), resid, tiles)

    def more(state):
        return state[0][0] < most[0]

    def again(state):
        first, base = state
        return first + depth, add_round(first, base, tiles)[0]

    return lax.while_loop(more, again, (jnp.full((1,), depth, jnp.int32), out))[1]


def solution(mesh):
    in_specs = (P("occ", "vir", None), P("occ", "vir", None), P("vir", "occ", None), P(), P(), P())
    out_specs = P("occ", "vir", None)
    body = functools.partial(shards, mesh.shape["occ"], mesh.shape["vir"])
    return jax.shard_map(body, mesh=mesh, in_specs=in_specs, out_specs=out_specs, check_vma=False)
```

```python
import functools

import jax
import jax.numpy as jnp
from jax import lax
from jax.experimental import pallas as pl
from jax.experimental.pallas import tpu as pltpu
from jax.sharding import PartitionSpec as P

GROUP = 8
LANES = 128
DEPTH = 192

NT = (((1,), (1,)), ((), ()))
NN = (((1,), (0,)), ((), ()))


def dot(left, right, dims):
    return lax.dot_general(left, right, dims, preferred_element_type=jnp.float32)


def split(values):
    high = values.astype(jnp.bfloat16)
    return high, (values - high.astype(jnp.float32)).astype(jnp.bfloat16)


def iota(shape, dim):
    return lax.broadcasted_iota(jnp.int32, shape, dim)


def pair_rows(firsts, seconds, width):
    tile = firsts.shape[1]
    column, orbital = iota((tile, width), 1), iota((tile, width), 0)
    outer = (lax.div(column, tile) == orbital).astype(jnp.bfloat16)
    inner = (lax.rem(column, tile) == orbital).astype(jnp.bfloat16)
    spread = lambda rows, how: dot(rows.astype(jnp.float32).astype(jnp.bfloat16), how, NN).astype(jnp.int32)
    return jnp.bitwise_xor(spread(firsts, outer), spread(seconds, inner))


def ranks(irrep):
    width = irrep.shape[1]
    member = (irrep == iota(irrep.shape, 0)).astype(jnp.float32)
    parts = [member[:, at : at + LANES] for at in range(0, width, LANES)]
    before = (iota((LANES, LANES), 0) < iota((LANES, LANES), 1)).astype(jnp.bfloat16)
    inside = dot(jnp.concatenate(parts, axis=0).astype(jnp.bfloat16), before, NN)
    base = jnp.zeros((GROUP, 1), jnp.float32)
    out = []
    for place, part in enumerate(parts):
        count = inside[place * GROUP : (place + 1) * GROUP] + base
        out.append(jnp.sum(part * count, axis=0, keepdims=True))
        base = base + jnp.sum(part, axis=1, keepdims=True)
    return jnp.concatenate(out, axis=1).astype(jnp.int32)


def prep_kernel(depth, first_ref, tasks_ref, pairs_ref, irreps_ref, ints_ref, buf_ref, meta_ref):
    own, block = lax.axis_index("vir"), lax.axis_index("occ")
    height, width = ints_ref.shape
    tile = irreps_ref.shape[1]
    first = first_ref[0]
    cd = tasks_ref[own]
    row = lambda pair, side: irreps_ref[pl.ds(pairs_ref[pair, side], 1), :]
    wide = lambda values: jnp.broadcast_to(values, (GROUP, tile))
    ab_outer, ab_inner = row(own, 0), row(own, 1)
    irrep = pair_rows(
        jnp.concatenate([wide(row(cd, 0)), wide(ab_outer)], axis=0),
        jnp.concatenate([wide(row(cd, 1)), wide(ab_inner)], axis=0),
        width,
    )
    cd_irrep, ab_irrep = irrep[:GROUP], irrep[GROUP:]
    rank = ranks(cd_irrep) - first
    inside = jnp.logical_and(rank >= 0, rank < depth)
    slot = jnp.where(inside, cd_irrep[:1] * depth + rank, -1)
    meta_ref[...] = jnp.where(iota((GROUP, width), 0) == 0, jnp.broadcast_to(slot, (GROUP, width)), ab_irrep)
    pair = iota((height, tile), 0) + block * height
    lane = iota((height, tile), 1)
    outer = jnp.sum(jnp.where(lane == lax.div(pair, tile), ab_outer, 0), axis=1, keepdims=True)
    inner = jnp.sum(jnp.where(lane == lax.rem(pair, tile), ab_inner, 0), axis=1, keepdims=True)
    live = jnp.bitwise_xor(outer, inner) == cd_irrep[:1]
    high, low = split(jnp.where(live, ints_ref[...], 0.0))
    pick = (iota((depth, width), 0) == rank).astype(jnp.bfloat16)
    buf_ref[...] = dot(pick, high, NT) + dot(pick, low, NT)


def prep(first, tasks, pairs, irreps, ints, depth):
    height, width = ints.shape
    smem, vmem = pl.BlockSpec(memory_space=pltpu.SMEM), pl.BlockSpec(memory_space=pltpu.VMEM)
    return pl.pallas_call(
        functools.partial(prep_kernel, depth),
        out_shape=(
            jax.ShapeDtypeStruct((depth, height), jnp.float32),
            jax.ShapeDtypeStruct((GROUP, width), jnp.int32),
        ),
        in_specs=[smem, smem, smem, vmem, vmem],
        out_specs=(vmem, vmem),
        compiler_params=pltpu.CompilerParams(vmem_limit_bytes=32 << 20),
        cost_estimate=pl.CostEstimate(flops=4 * depth * height * width, bytes_accessed=4 * height * width, transcendentals=0),
        name="compact",
    )(first, tasks, pairs, irreps, ints)


def count_kernel(width, tasks_ref, pairs_ref, irreps_ref, most_ref):
    rows = lambda side: jnp.concatenate(
        [irreps_ref[pl.ds(pairs_ref[tasks_ref[k], side], 1), :] for k in range(tasks_ref.shape[0])], axis=0
    )
    irrep = pair_rows(rows(0), rows(1), width)
    most = jnp.zeros((irrep.shape[0], 1), jnp.int32)
    for g in range(GROUP):
        most = jnp.maximum(most, jnp.sum((irrep == g).astype(jnp.int32), axis=1, keepdims=True))
    most_ref[0] = jnp.max(most)


def count(tasks, pairs, irreps, width):
    smem, vmem = pl.BlockSpec(memory_space=pltpu.SMEM), pl.BlockSpec(memory_space=pltpu.VMEM)
    return pl.pallas_call(
        functools.partial(count_kernel, width),
        out_shape=jax.ShapeDtypeStruct((1,), jnp.int32),
        in_specs=[smem, smem, vmem],
        out_specs=smem,
        name="count",
    )(tasks, pairs, irreps)


def order_kernel(depth, count, *refs):
    tasks_ref, meta_ref = refs[:2]
    tiles, (out_ref, held, sem) = refs[2 : 2 + count], refs[2 + count :]
    own = lax.axis_index("vir")
    chosen = jnp.bitwise_xor(tasks_ref[own], own)
    copies = [pltpu.make_async_copy(tile_ref.at[:, 0, :], held, sem) for tile_ref in tiles]
    for number, copy in enumerate(copies):
        pl.when(chosen == number)(copy.start)
    width, size = meta_ref.shape[1], GROUP * depth // 4
    starts = range(0, GROUP * depth, size)
    places = [(iota((size, width), 0) + at == meta_ref[:1]).astype(jnp.bfloat16) for at in starts]
    copies[0].wait()
    both = jnp.concatenate(split(held[...]), axis=0)
    for at, place in zip(starts, places):
        out_ref[:, at : at + size] = dot(both, place, NT).astype(jnp.bfloat16)


def order(tasks, meta, tiles, depth):
    height, _, width = tiles[0].shape
    smem, vmem = pl.BlockSpec(memory_space=pltpu.SMEM), pl.BlockSpec(memory_space=pltpu.VMEM)
    return pl.pallas_call(
        functools.partial(order_kernel, depth, len(tiles)),
        out_shape=jax.ShapeDtypeStruct((2 * height, GROUP * depth), jnp.bfloat16),
        in_specs=[smem, vmem] + [pl.BlockSpec(memory_space=pl.ANY)] * len(tiles),
        out_specs=vmem,
        scratch_shapes=[pltpu.VMEM((height, width), jnp.float32), pltpu.SemaphoreType.DMA],
        compiler_params=pltpu.CompilerParams(vmem_limit_bytes=32 << 20),
        cost_estimate=pl.CostEstimate(
            flops=4 * height * width * GROUP * depth, bytes_accessed=4 * height * width, transcendentals=0
        ),
        name="order_amplitudes",
    )(tasks, meta, *tiles)


def ladder_kernel(depth, masks, count, meta_ref, amps_ref, *refs):
    pieces, base_ref, (out_ref, held, sems) = refs[:count], refs[count], refs[-3:]
    block = lax.axis_index("occ")
    height = held.shape[0]
    size = pieces[0].shape[1]
    pieces = [piece.at[at : at + depth] for piece in pieces for at in range(0, piece.shape[0], depth)]
    places = [pl.ds(pl.multiple_of(jnp.bitwise_xor(block, mask) * size, LANES), size) for mask in masks]
    loads = [
        pltpu.make_async_copy(base_ref.at[:, 0, place], held.at[:, n * size : (n + 1) * size], sems.at[n])
        for n, place in enumerate(places)
    ]
    for load in loads:
        load.start()
    high, low = split(jnp.concatenate([piece[...] for piece in pieces], axis=1))
    irrep = jnp.concatenate([meta_ref[1:2, place] for place in places], axis=1)
    zero = jnp.zeros((), jnp.bfloat16)
    blocks = lambda values: jnp.concatenate([jnp.where(irrep == g, values, zero) for g in range(GROUP)], axis=0)
    both = dot(amps_ref[...], blocks(high), NN)
    ladder = both[:height] + both[height:] + dot(amps_ref[:height], blocks(low), NN)
    for load in loads:
        load.wait()
    held[...] += ladder
    stores = [
        pltpu.make_async_copy(held.at[:, n * size : (n + 1) * size], out_ref.at[:, 0, place], sems.at[n])
        for n, place in enumerate(places)
    ]
    for store in stores:
        store.start()
    for store in stores:
        store.wait()


def ladder(meta, amps, masks, pieces, base, out, depth):
    into = () if out is None else (out,)
    height, size = base.shape[0], pieces[0].shape[1]
    vmem, hbm = pl.BlockSpec(memory_space=pltpu.VMEM), pl.BlockSpec(memory_space=pl.ANY)
    columns = size * len(masks)
    return pl.pallas_call(
        functools.partial(ladder_kernel, depth, masks, len(pieces)),
        out_shape=jax.ShapeDtypeStruct(base.shape, base.dtype),
        in_specs=[vmem, vmem] + [vmem] * len(pieces) + [hbm] * (1 + len(into)),
        out_specs=hbm,
        scratch_shapes=[pltpu.VMEM((height, columns), jnp.float32), pltpu.SemaphoreType.DMA((len(masks),))],
        input_output_aliases={3 + len(pieces): 0} if into else {},
        compiler_params=pltpu.CompilerParams(vmem_limit_bytes=48 << 20),
        cost_estimate=pl.CostEstimate(
            flops=6 * height * columns * GROUP * depth, bytes_accessed=8 * height * columns, transcendentals=0
        ),
        name="ladder",
    )(meta, amps, *pieces, base, *into)


def swap(values, axis, size, mask):
    return lax.ppermute(values, axis, [(device, device ^ mask) for device in range(size)])


def first_swaps(amps, size):
    return {0: amps, size >> 1: swap(amps, "vir", size, size >> 1)}


def other_swaps(tiles, size):
    bit = size >> 2
    while bit:
        for number in sorted(tiles):
            tiles[number | bit] = swap(tiles[number], "vir", size, bit)
        bit >>= 1
    return [tiles[number] for number in range(size)]


def after(value, earlier):
    return lax.optimization_barrier((value, earlier))[0]


def exchange(buf, size):
    lead = size >> 1
    even = [lead] + [mask for mask in range(2, size, 2) if mask != lead] if size > 2 else []
    near = {0: buf}
    for mask in even:
        near[mask] = swap(buf, "occ", size, mask) if mask <= lead else swap(near[mask & (mask - 1)], "occ", size, mask & -mask)
    blocks = {(mask,): piece for mask, piece in near.items()}
    groups = [(0,), tuple(even[-2::-1]), tuple(even[-1:])] if size > 1 else []
    for group in groups:
        if group:
            whole = jnp.concatenate([near[mask] for mask in group], axis=0) if len(group) > 1 else near[group[0]]
            blocks[tuple(mask | 1 for mask in group)] = swap(whole, "occ", size, 1)
    return blocks, [piece for masks, piece in blocks.items() if len(masks) == 1 and masks[0] <= lead]


def shards(occ_size, vir_size, amps, resid, ints, tasks, pair_tiles, irreps):
    rows = ints[0]
    height, width = rows.shape
    depth = min(DEPTH, width)

    def add_round(first, base):
        tiles = first_swaps(amps, vir_size)
        buf, meta = prep(first, tasks, pair_tiles, irreps, rows, depth)
        if height % LANES or occ_size & (occ_size - 1):
            blocks = {(0,): lax.all_gather(buf, "occ", axis=1, tiled=True)}
            tiles = other_swaps(tiles, vir_size)
        else:
            blocks, direct = exchange(buf, occ_size)
            tiles = {number: after(tile, direct) if number else tile for number, tile in tiles.items()}
            tiles = other_swaps(tiles, vir_size)
        tiles, base = lax.optimization_barrier((tiles, base))
        ordered = order(tasks, meta, tiles, depth)
        return ladder(meta, ordered, sum(blocks, ()), list(blocks.values()), base, None, depth)

    most = count(tasks, pair_tiles, irreps, width)
    rest = lax.while_loop(
        lambda state: state[0][0] < most[0],
        lambda state: (state[0] + depth, add_round(*state)),
        (jnp.full((1,), depth, jnp.int32), resid),
    )[1]
    return add_round(jnp.zeros((1,), jnp.int32), rest)


def solution(mesh):
    in_specs = (P("occ", "vir", None), P("occ", "vir", None), P("vir", "occ", None), P(), P(), P())
    out_specs = P("occ", "vir", None)
    body = functools.partial(shards, mesh.shape["occ"], mesh.shape["vir"])
    return jax.shard_map(body, mesh=mesh, in_specs=in_specs, out_specs=out_specs, check_vma=False)
```

```python
import functools

import jax
import jax.numpy as jnp
from jax import lax
from jax.experimental import pallas as pl
from jax.experimental.pallas import tpu as pltpu
from jax.sharding import PartitionSpec as P

GROUP = 8
LANES = 128
DEPTH = 176

NT = (((1,), (1,)), ((), ()))
NN = (((1,), (0,)), ((), ()))


def dot(left, right, dims):
    return lax.dot_general(left, right, dims, preferred_element_type=jnp.float32)


def split(values):
    high = values.astype(jnp.bfloat16)
    return high, (values - high.astype(jnp.float32)).astype(jnp.bfloat16)


def iota(shape, dim):
    return lax.broadcasted_iota(jnp.int32, shape, dim)


def pair_rows(firsts, seconds, width):
    tile = firsts.shape[1]
    column, orbital = iota((tile, width), 1), iota((tile, width), 0)
    outer = (lax.div(column, tile) == orbital).astype(jnp.bfloat16)
    inner = (lax.rem(column, tile) == orbital).astype(jnp.bfloat16)
    spread = lambda rows, how: dot(rows.astype(jnp.float32).astype(jnp.bfloat16), how, NN).astype(jnp.int32)
    return jnp.bitwise_xor(spread(firsts, outer), spread(seconds, inner))


def ranks(irrep):
    width = irrep.shape[1]
    member = (irrep == iota(irrep.shape, 0)).astype(jnp.float32)
    parts = [member[:, at : at + LANES] for at in range(0, width, LANES)]
    before = (iota((LANES, LANES), 0) < iota((LANES, LANES), 1)).astype(jnp.bfloat16)
    inside = dot(jnp.concatenate(parts, axis=0).astype(jnp.bfloat16), before, NN)
    base = jnp.zeros((GROUP, 1), jnp.float32)
    out = []
    for place, part in enumerate(parts):
        count = inside[place * GROUP : (place + 1) * GROUP] + base
        out.append(jnp.sum(part * count, axis=0, keepdims=True))
        base = base + jnp.sum(part, axis=1, keepdims=True)
    return jnp.concatenate(out, axis=1).astype(jnp.int32)


def prep_kernel(depth, first_ref, tasks_ref, pairs_ref, irreps_ref, ints_ref, buf_ref, meta_ref):
    own, block = lax.axis_index("vir"), lax.axis_index("occ")
    height, width = ints_ref.shape
    tile = irreps_ref.shape[1]
    first = first_ref[0]
    cd = tasks_ref[own]
    row = lambda pair, side: irreps_ref[pl.ds(pairs_ref[pair, side], 1), :]
    wide = lambda values: jnp.broadcast_to(values, (GROUP, tile))
    ab_outer, ab_inner = row(own, 0), row(own, 1)
    irrep = pair_rows(
        jnp.concatenate([wide(row(cd, 0)), wide(ab_outer)], axis=0),
        jnp.concatenate([wide(row(cd, 1)), wide(ab_inner)], axis=0),
        width,
    )
    cd_irrep, ab_irrep = irrep[:GROUP], irrep[GROUP:]
    rank = ranks(cd_irrep) - first
    inside = jnp.logical_and(rank >= 0, rank < depth)
    slot = jnp.where(inside, cd_irrep[:1] * depth + rank, -1)
    meta_ref[...] = jnp.where(iota((GROUP, width), 0) == 0, jnp.broadcast_to(slot, (GROUP, width)), ab_irrep)
    pair = iota((height, tile), 0) + block * height
    lane = iota((height, tile), 1)
    outer = jnp.sum(jnp.where(lane == lax.div(pair, tile), ab_outer, 0), axis=1, keepdims=True)
    inner = jnp.sum(jnp.where(lane == lax.rem(pair, tile), ab_inner, 0), axis=1, keepdims=True)
    live = jnp.bitwise_xor(outer, inner) == cd_irrep[:1]
    high, low = split(jnp.where(live, ints_ref[...], 0.0))
    pick = (iota((depth, width), 0) == rank).astype(jnp.bfloat16)
    buf_ref[...] = dot(pick, high, NT) + dot(pick, low, NT)


def prep(first, tasks, pairs, irreps, ints, depth):
    height, width = ints.shape
    smem, vmem = pl.BlockSpec(memory_space=pltpu.SMEM), pl.BlockSpec(memory_space=pltpu.VMEM)
    return pl.pallas_call(
        functools.partial(prep_kernel, depth),
        out_shape=(
            jax.ShapeDtypeStruct((depth, height), jnp.float32),
            jax.ShapeDtypeStruct((GROUP, width), jnp.int32),
        ),
        in_specs=[smem, smem, smem, vmem, vmem],
        out_specs=(vmem, vmem),
        compiler_params=pltpu.CompilerParams(vmem_limit_bytes=32 << 20),
        cost_estimate=pl.CostEstimate(flops=4 * depth * height * width, bytes_accessed=4 * height * width, transcendentals=0),
        name="compact",
    )(first, tasks, pairs, irreps, ints)


def count_kernel(width, tasks_ref, pairs_ref, irreps_ref, most_ref):
    rows = lambda side: jnp.concatenate(
        [irreps_ref[pl.ds(pairs_ref[tasks_ref[k], side], 1), :] for k in range(tasks_ref.shape[0])], axis=0
    )
    irrep = pair_rows(rows(0), rows(1), width)
    most = jnp.zeros((irrep.shape[0], 1), jnp.int32)
    for g in range(GROUP):
        most = jnp.maximum(most, jnp.sum((irrep == g).astype(jnp.int32), axis=1, keepdims=True))
    most_ref[0] = jnp.max(most)


def count(tasks, pairs, irreps, width):
    smem, vmem = pl.BlockSpec(memory_space=pltpu.SMEM), pl.BlockSpec(memory_space=pltpu.VMEM)
    return pl.pallas_call(
        functools.partial(count_kernel, width),
        out_shape=jax.ShapeDtypeStruct((1,), jnp.int32),
        in_specs=[smem, smem, vmem],
        out_specs=smem,
        name="count",
    )(tasks, pairs, irreps)


def order_kernel(depth, count, *refs):
    tasks_ref, meta_ref = refs[:2]
    tiles, (out_ref, held, sem) = refs[2 : 2 + count], refs[2 + count :]
    own = lax.axis_index("vir")
    chosen = jnp.bitwise_xor(tasks_ref[own], own)
    copies = [pltpu.make_async_copy(tile_ref.at[:, 0, :], held, sem) for tile_ref in tiles]
    for number, copy in enumerate(copies):
        pl.when(chosen == number)(copy.start)
    width, slots, size = meta_ref.shape[1], GROUP * depth, 3 * LANES
    starts = range(0, slots, size)
    places = [(iota((min(size, slots - at), width), 0) + at == meta_ref[:1]).astype(jnp.bfloat16) for at in starts]
    copies[0].wait()
    both = jnp.concatenate(split(held[...]), axis=0)
    for at, place in zip(starts, places):
        out_ref[:, at : at + place.shape[0]] = dot(both, place, NT).astype(jnp.bfloat16)


def order(tasks, meta, tiles, depth):
    height, _, width = tiles[0].shape
    smem, vmem = pl.BlockSpec(memory_space=pltpu.SMEM), pl.BlockSpec(memory_space=pltpu.VMEM)
    return pl.pallas_call(
        functools.partial(order_kernel, depth, len(tiles)),
        out_shape=jax.ShapeDtypeStruct((2 * height, GROUP * depth), jnp.bfloat16),
        in_specs=[smem, vmem] + [pl.BlockSpec(memory_space=pltpu.HBM)] * len(tiles),
        out_specs=vmem,
        scratch_shapes=[pltpu.VMEM((height, width), jnp.float32), pltpu.SemaphoreType.DMA],
        compiler_params=pltpu.CompilerParams(vmem_limit_bytes=32 << 20),
        cost_estimate=pl.CostEstimate(
            flops=40 * height * width * GROUP * depth, bytes_accessed=4 * height * width, transcendentals=0
        ),
        name="order_amplitudes",
    )(tasks, meta, *tiles)


def ladder_kernel(depth, masks, count, meta_ref, amps_ref, *refs):
    pieces, base_ref, (out_ref, held, sems) = refs[:count], refs[count], refs[-3:]
    block = lax.axis_index("occ")
    height = held.shape[0]
    size = pieces[0].shape[1]
    pieces = [piece.at[at : at + depth] for piece in pieces for at in range(0, piece.shape[0], depth)]
    places = [pl.ds(pl.multiple_of(jnp.bitwise_xor(block, mask) * size, LANES), size) for mask in masks]
    loads = [
        pltpu.make_async_copy(base_ref.at[:, 0, place], held.at[:, n * size : (n + 1) * size], sems.at[n])
        for n, place in enumerate(places)
    ]
    for load in loads:
        load.start()
    high, low = split(jnp.concatenate([piece[...] for piece in pieces], axis=1))
    irrep = jnp.concatenate([meta_ref[1:2, place] for place in places], axis=1)
    zero = jnp.zeros((), jnp.bfloat16)
    blocks = lambda values: jnp.concatenate([jnp.where(irrep == g, values, zero) for g in range(GROUP)], axis=0)
    both = dot(amps_ref[...], blocks(high), NN)
    ladder = both[:height] + both[height:] + dot(amps_ref[:height], blocks(low), NN)
    for load in loads:
        load.wait()
    held[...] += ladder
    stores = [
        pltpu.make_async_copy(held.at[:, n * size : (n + 1) * size], out_ref.at[:, 0, place], sems.at[n])
        for n, place in enumerate(places)
    ]
    for store in stores:
        store.start()
    for store in stores:
        store.wait()


def ladder(meta, amps, masks, pieces, base, out, depth):
    into = () if out is None else (out,)
    height, size = base.shape[0], pieces[0].shape[1]
    vmem, hbm = pl.BlockSpec(memory_space=pltpu.VMEM), pl.BlockSpec(memory_space=pl.ANY)
    columns = size * len(masks)
    return pl.pallas_call(
        functools.partial(ladder_kernel, depth, masks, len(pieces)),
        out_shape=jax.ShapeDtypeStruct(base.shape, base.dtype),
        in_specs=[vmem, vmem] + [vmem] * len(pieces) + [hbm] * (1 + len(into)),
        out_specs=hbm,
        scratch_shapes=[pltpu.VMEM((height, columns), jnp.float32), pltpu.SemaphoreType.DMA((len(masks),))],
        input_output_aliases={3 + len(pieces): 0} if into else {},
        compiler_params=pltpu.CompilerParams(vmem_limit_bytes=48 << 20),
        cost_estimate=pl.CostEstimate(
            flops=6 * height * columns * GROUP * depth, bytes_accessed=8 * height * columns, transcendentals=0
        ),
        name="ladder",
    )(meta, amps, *pieces, base, *into)


def swap(values, axis, size, mask):
    return lax.ppermute(values, axis, [(device, device ^ mask) for device in range(size)])


def first_swaps(amps, size):
    return {0: amps, size >> 1: swap(amps, "vir", size, size >> 1)}


def other_swaps(tiles, size):
    bit = size >> 2
    while bit:
        for number in sorted(tiles):
            tiles[number | bit] = swap(tiles[number], "vir", size, bit)
        bit >>= 1
    return [tiles[number] for number in range(size)]


def after(value, earlier):
    return lax.optimization_barrier((value, earlier))[0]


def exchange(buf, size):
    lead = size >> 1
    even = [lead] + [mask for mask in range(2, size, 2) if mask != lead] if size > 2 else []
    near = {0: buf}
    for mask in even:
        near[mask] = swap(buf, "occ", size, mask) if mask <= lead else swap(near[mask & (mask - 1)], "occ", size, mask & -mask)
    blocks = {(mask,): piece for mask, piece in near.items()}
    groups = [(0,), tuple(even[-2::-1]), tuple(even[-1:])] if size > 1 else []
    for group in groups:
        if group:
            whole = jnp.concatenate([near[mask] for mask in group], axis=0) if len(group) > 1 else near[group[0]]
            blocks[tuple(mask | 1 for mask in group)] = swap(whole, "occ", size, 1)
    return blocks, [piece for masks, piece in blocks.items() if len(masks) == 1 and masks[0] <= lead]


def shards(occ_size, vir_size, amps, resid, ints, tasks, pair_tiles, irreps):
    rows = ints[0]
    height, width = rows.shape
    depth = min(DEPTH, width)

    def add_round(first, base):
        tiles = first_swaps(amps, vir_size)
        buf, meta = prep(first, tasks, pair_tiles, irreps, rows, depth)
        if height % LANES or occ_size & (occ_size - 1):
            blocks = {(0,): lax.all_gather(buf, "occ", axis=1, tiled=True)}
            tiles = other_swaps(tiles, vir_size)
        else:
            blocks, direct = exchange(buf, occ_size)
            tiles = {number: after(tile, direct) if number else tile for number, tile in tiles.items()}
            tiles = other_swaps(tiles, vir_size)
        tiles, base = lax.optimization_barrier((tiles, base))
        ordered = order(tasks, meta, tiles, depth)
        return ladder(meta, ordered, sum(blocks, ()), list(blocks.values()), base, None, depth)

    most = count(tasks, pair_tiles, irreps, width)
    rest = lax.while_loop(
        lambda state: state[0][0] < most[0],
        lambda state: (state[0] + depth, add_round(*state)),
        (jnp.full((1,), depth, jnp.int32), resid),
    )[1]
    return add_round(jnp.zeros((1,), jnp.int32), rest)


def solution(mesh):
    in_specs = (P("occ", "vir", None), P("occ", "vir", None), P("vir", "occ", None), P(), P(), P())
    out_specs = P("occ", "vir", None)
    body = functools.partial(shards, mesh.shape["occ"], mesh.shape["vir"])
    return jax.shard_map(body, mesh=mesh, in_specs=in_specs, out_specs=out_specs, check_vma=False)
```

```python
import functools

import jax
import jax.numpy as jnp
from jax import lax
from jax.experimental import pallas as pl
from jax.experimental.pallas import tpu as pltpu
from jax.sharding import PartitionSpec as P

GROUP = 8
LANES = 128
DEPTH = 176

NT = (((1,), (1,)), ((), ()))
NN = (((1,), (0,)), ((), ()))


def dot(left, right, dims):
    return lax.dot_general(left, right, dims, preferred_element_type=jnp.float32)


def split(values):
    high = values.astype(jnp.bfloat16)
    return high, (values - high.astype(jnp.float32)).astype(jnp.bfloat16)


def iota(shape, dim):
    return lax.broadcasted_iota(jnp.int32, shape, dim)


def pair_rows(firsts, seconds, width):
    tile = firsts.shape[1]
    column, orbital = iota((tile, width), 1), iota((tile, width), 0)
    outer = (lax.div(column, tile) == orbital).astype(jnp.bfloat16)
    inner = (lax.rem(column, tile) == orbital).astype(jnp.bfloat16)
    spread = lambda rows, how: dot(rows.astype(jnp.float32).astype(jnp.bfloat16), how, NN).astype(jnp.int32)
    return jnp.bitwise_xor(spread(firsts, outer), spread(seconds, inner))


def ranks(irrep):
    width = irrep.shape[1]
    member = (irrep == iota(irrep.shape, 0)).astype(jnp.float32)
    parts = [member[:, at : at + LANES] for at in range(0, width, LANES)]
    before = (iota((LANES, LANES), 0) < iota((LANES, LANES), 1)).astype(jnp.bfloat16)
    inside = dot(jnp.concatenate(parts, axis=0).astype(jnp.bfloat16), before, NN)
    base = jnp.zeros((GROUP, 1), jnp.float32)
    out = []
    for place, part in enumerate(parts):
        count = inside[place * GROUP : (place + 1) * GROUP] + base
        out.append(jnp.sum(part * count, axis=0, keepdims=True))
        base = base + jnp.sum(part, axis=1, keepdims=True)
    return jnp.concatenate(out, axis=1).astype(jnp.int32)


def prep_kernel(depth, first_ref, tasks_ref, pairs_ref, irreps_ref, ints_ref, buf_ref, meta_ref):
    own, block = lax.axis_index("vir"), lax.axis_index("occ")
    height, width = ints_ref.shape
    tile = irreps_ref.shape[1]
    first = first_ref[0]
    cd = tasks_ref[own]
    row = lambda pair, side: irreps_ref[pl.ds(pairs_ref[pair, side], 1), :]
    wide = lambda values: jnp.broadcast_to(values, (GROUP, tile))
    ab_outer, ab_inner = row(own, 0), row(own, 1)
    irrep = pair_rows(
        jnp.concatenate([wide(row(cd, 0)), wide(ab_outer)], axis=0),
        jnp.concatenate([wide(row(cd, 1)), wide(ab_inner)], axis=0),
        width,
    )
    cd_irrep, ab_irrep = irrep[:GROUP], irrep[GROUP:]
    rank = ranks(cd_irrep) - first
    inside = jnp.logical_and(rank >= 0, rank < depth)
    slot = jnp.where(inside, cd_irrep[:1] * depth + rank, -1)
    meta_ref[...] = jnp.where(iota((GROUP, width), 0) == 0, jnp.broadcast_to(slot, (GROUP, width)), ab_irrep)
    pair = iota((height, tile), 0) + block * height
    lane = iota((height, tile), 1)
    outer = jnp.sum(jnp.where(lane == lax.div(pair, tile), ab_outer, 0), axis=1, keepdims=True)
    inner = jnp.sum(jnp.where(lane == lax.rem(pair, tile), ab_inner, 0), axis=1, keepdims=True)
    live = jnp.bitwise_xor(outer, inner) == cd_irrep[:1]
    high, low = split(jnp.where(live, ints_ref[...], 0.0))
    pick = (iota((depth, width), 0) == rank).astype(jnp.bfloat16)
    buf_ref[...] = dot(pick, high, NT) + dot(pick, low, NT)


def prep(first, tasks, pairs, irreps, ints, depth):
    height, width = ints.shape
    smem, vmem = pl.BlockSpec(memory_space=pltpu.SMEM), pl.BlockSpec(memory_space=pltpu.VMEM)
    return pl.pallas_call(
        functools.partial(prep_kernel, depth),
        out_shape=(
            jax.ShapeDtypeStruct((depth, height), jnp.float32),
            jax.ShapeDtypeStruct((GROUP, width), jnp.int32),
        ),
        in_specs=[smem, smem, smem, vmem, vmem],
        out_specs=(vmem, vmem),
        compiler_params=pltpu.CompilerParams(vmem_limit_bytes=32 << 20),
        cost_estimate=pl.CostEstimate(flops=4 * depth * height * width, bytes_accessed=4 * height * width, transcendentals=0),
        name="compact",
    )(first, tasks, pairs, irreps, ints)


def count_kernel(width, tasks_ref, pairs_ref, irreps_ref, most_ref):
    rows = lambda side: jnp.concatenate(
        [irreps_ref[pl.ds(pairs_ref[tasks_ref[k], side], 1), :] for k in range(tasks_ref.shape[0])], axis=0
    )
    irrep = pair_rows(rows(0), rows(1), width)
    most = jnp.zeros((irrep.shape[0], 1), jnp.int32)
    for g in range(GROUP):
        most = jnp.maximum(most, jnp.sum((irrep == g).astype(jnp.int32), axis=1, keepdims=True))
    most_ref[0] = jnp.max(most)


def count(tasks, pairs, irreps, width):
    smem, vmem = pl.BlockSpec(memory_space=pltpu.SMEM), pl.BlockSpec(memory_space=pltpu.VMEM)
    return pl.pallas_call(
        functools.partial(count_kernel, width),
        out_shape=jax.ShapeDtypeStruct((1,), jnp.int32),
        in_specs=[smem, smem, vmem],
        out_specs=smem,
        name="count",
    )(tasks, pairs, irreps)


def order_kernel(depth, count, *refs):
    tasks_ref, meta_ref = refs[:2]
    tiles, (out_ref, held, sem) = refs[2 : 2 + count], refs[2 + count :]
    own = lax.axis_index("vir")
    chosen = jnp.bitwise_xor(tasks_ref[own], own)
    copies = [pltpu.make_async_copy(tile_ref.at[:, 0, :], held, sem) for tile_ref in tiles]
    for number, copy in enumerate(copies):
        pl.when(chosen == number)(copy.start)
    width, slots, size = meta_ref.shape[1], GROUP * depth, 3 * LANES
    starts = range(0, slots, size)
    places = [(iota((min(size, slots - at), width), 0) + at == meta_ref[:1]).astype(jnp.bfloat16) for at in starts]
    copies[0].wait()
    both = jnp.concatenate(split(held[...]), axis=0)
    for at, place in zip(starts, places):
        out_ref[:, at : at + place.shape[0]] = dot(both, place, NT).astype(jnp.bfloat16)


def order(tasks, meta, tiles, depth):
    height, _, width = tiles[0].shape
    smem, vmem = pl.BlockSpec(memory_space=pltpu.SMEM), pl.BlockSpec(memory_space=pltpu.VMEM)
    return pl.pallas_call(
        functools.partial(order_kernel, depth, len(tiles)),
        out_shape=jax.ShapeDtypeStruct((2 * height, GROUP * depth), jnp.bfloat16),
        in_specs=[smem, vmem] + [pl.BlockSpec(memory_space=pltpu.HBM)] * len(tiles),
        out_specs=vmem,
        scratch_shapes=[pltpu.VMEM((height, width), jnp.float32), pltpu.SemaphoreType.DMA],
        compiler_params=pltpu.CompilerParams(vmem_limit_bytes=32 << 20),
        cost_estimate=pl.CostEstimate(
            flops=40 * height * width * GROUP * depth, bytes_accessed=4 * height * width, transcendentals=0
        ),
        name="order_amplitudes",
    )(tasks, meta, *tiles)


def ladder_kernel(depth, masks, count, meta_ref, amps_ref, *refs):
    pieces, (base_ref, out_ref, held, load_sem, store_sem) = refs[:count], refs[count:]
    block = lax.axis_index("occ")
    height, width = held.shape
    size = pieces[0].shape[1]
    pieces = [piece.at[at : at + depth] for piece in pieces for at in range(0, piece.shape[0], depth)]
    if size == width:
        places = [pl.ds(0, size)]
    else:
        places = [pl.ds(pl.multiple_of(jnp.bitwise_xor(block, mask) * size, LANES), size) for mask in masks]
    load = pltpu.make_async_copy(base_ref.at[:, 0, :], held, load_sem)
    load.start()
    high, low = split(jnp.concatenate([piece[...] for piece in pieces], axis=1))
    irrep = jnp.concatenate([meta_ref[1:2, place] for place in places], axis=1)
    zero = jnp.zeros((), jnp.bfloat16)
    blocks = lambda values: jnp.concatenate([jnp.where(irrep == g, values, zero) for g in range(GROUP)], axis=0)
    both = dot(amps_ref[...], blocks(high), NN)
    ladder = both[:height] + both[height:] + dot(amps_ref[:height], blocks(low), NN)
    load.wait()
    for n, place in enumerate(places):
        held[:, place] += ladder[:, n * size : (n + 1) * size]
    store = pltpu.make_async_copy(held, out_ref.at[:, 0, :], store_sem)
    store.start()
    store.wait()


def ladder(meta, amps, masks, pieces, base, depth):
    height, _, width = base.shape
    vmem, hbm = pl.BlockSpec(memory_space=pltpu.VMEM), pl.BlockSpec(memory_space=pl.ANY)
    return pl.pallas_call(
        functools.partial(ladder_kernel, depth, masks, len(pieces)),
        out_shape=jax.ShapeDtypeStruct(base.shape, base.dtype),
        in_specs=[vmem, vmem] + [vmem] * len(pieces) + [hbm],
        out_specs=hbm,
        scratch_shapes=[pltpu.VMEM((height, width), jnp.float32), pltpu.SemaphoreType.DMA, pltpu.SemaphoreType.DMA],
        compiler_params=pltpu.CompilerParams(vmem_limit_bytes=48 << 20),
        cost_estimate=pl.CostEstimate(
            flops=6 * height * width * GROUP * depth, bytes_accessed=8 * height * width, transcendentals=0
        ),
        name="ladder",
    )(meta, amps, *pieces, base)


def swap(values, axis, size, mask):
    return lax.ppermute(values, axis, [(device, device ^ mask) for device in range(size)])


def first_swaps(amps, size):
    return {0: amps, size >> 1: swap(amps, "vir", size, size >> 1)}


def other_swaps(tiles, size):
    bit = size >> 2
    while bit:
        for number in sorted(tiles):
            tiles[number | bit] = swap(tiles[number], "vir", size, bit)
        bit >>= 1
    return [tiles[number] for number in range(size)]


def after(value, earlier):
    return lax.optimization_barrier((value, earlier))[0]


def exchange(buf, size):
    lead = size >> 1
    even = [lead] + [mask for mask in range(2, size, 2) if mask != lead] if size > 2 else []
    near = {0: buf}
    for mask in even:
        near[mask] = swap(buf, "occ", size, mask) if mask <= lead else swap(near[mask & (mask - 1)], "occ", size, mask & -mask)
    blocks = {(mask,): piece for mask, piece in near.items()}
    groups = [(0,), tuple(even[-2::-1]), tuple(even[-1:])] if size > 1 else []
    for group in groups:
        if group:
            whole = jnp.concatenate([near[mask] for mask in group], axis=0) if len(group) > 1 else near[group[0]]
            blocks[tuple(mask | 1 for mask in group)] = swap(whole, "occ", size, 1)
    return blocks, [piece for masks, piece in blocks.items() if len(masks) == 1 and masks[0] <= lead]


def shards(occ_size, vir_size, amps, resid, ints, tasks, pair_tiles, irreps):
    rows = ints[0]
    height, width = rows.shape
    depth = min(DEPTH, width)

    def add_round(first, base):
        tiles = first_swaps(amps, vir_size)
        buf, meta = prep(first, tasks, pair_tiles, irreps, rows, depth)
        if height % LANES or occ_size & (occ_size - 1):
            blocks = {(0,): lax.all_gather(buf, "occ", axis=1, tiled=True)}
            tiles = other_swaps(tiles, vir_size)
        else:
            blocks, direct = exchange(buf, occ_size)
            tiles = {number: after(tile, direct) if number else tile for number, tile in tiles.items()}
            tiles = other_swaps(tiles, vir_size)
        tiles, base = lax.optimization_barrier((tiles, base))
        ordered = order(tasks, meta, tiles, depth)
        return ladder(meta, ordered, sum(blocks, ()), list(blocks.values()), base, depth)

    most = count(tasks, pair_tiles, irreps, width)
    rest = lax.while_loop(
        lambda state: state[0][0] < most[0],
        lambda state: (state[0] + depth, add_round(*state)),
        (jnp.full((1,), depth, jnp.int32), resid),
    )[1]
    return add_round(jnp.zeros((1,), jnp.int32), rest)


def solution(mesh):
    in_specs = (P("occ", "vir", None), P("occ", "vir", None), P("vir", "occ", None), P(), P(), P())
    out_specs = P("occ", "vir", None)
    body = functools.partial(shards, mesh.shape["occ"], mesh.shape["vir"])
    return jax.shard_map(body, mesh=mesh, in_specs=in_specs, out_specs=out_specs, check_vma=False)
```

```python
import functools

import jax
import jax.numpy as jnp
from jax import lax
from jax.experimental import pallas as pl
from jax.experimental.pallas import tpu as pltpu
from jax.sharding import PartitionSpec as P

GROUP = 8
LANES = 128
DEPTH = 176

NT = (((1,), (1,)), ((), ()))
NN = (((1,), (0,)), ((), ()))


def dot(left, right, dims):
    return lax.dot_general(left, right, dims, preferred_element_type=jnp.float32)


def split(values):
    high = values.astype(jnp.bfloat16)
    return high, (values - high.astype(jnp.float32)).astype(jnp.bfloat16)


def iota(shape, dim):
    return lax.broadcasted_iota(jnp.int32, shape, dim)


def pair_rows(firsts, seconds, width):
    tile = firsts.shape[1]
    column, orbital = iota((tile, width), 1), iota((tile, width), 0)
    outer = (lax.div(column, tile) == orbital).astype(jnp.bfloat16)
    inner = (lax.rem(column, tile) == orbital).astype(jnp.bfloat16)
    spread = lambda rows, how: dot(rows.astype(jnp.float32).astype(jnp.bfloat16), how, NN).astype(jnp.int32)
    return jnp.bitwise_xor(spread(firsts, outer), spread(seconds, inner))


def ranks(irrep):
    width = irrep.shape[1]
    member = (irrep == iota(irrep.shape, 0)).astype(jnp.float32)
    parts = [member[:, at : at + LANES] for at in range(0, width, LANES)]
    before = (iota((LANES, LANES), 0) < iota((LANES, LANES), 1)).astype(jnp.bfloat16)
    inside = dot(jnp.concatenate(parts, axis=0).astype(jnp.bfloat16), before, NN)
    base = jnp.zeros((GROUP, 1), jnp.float32)
    out = []
    for place, part in enumerate(parts):
        count = inside[place * GROUP : (place + 1) * GROUP] + base
        out.append(jnp.sum(part * count, axis=0, keepdims=True))
        base = base + jnp.sum(part, axis=1, keepdims=True)
    return jnp.concatenate(out, axis=1).astype(jnp.int32)


def prep_kernel(depth, first_ref, tasks_ref, pairs_ref, irreps_ref, ints_ref, buf_ref, meta_ref):
    own, block = lax.axis_index("vir"), lax.axis_index("occ")
    height, width = ints_ref.shape
    tile = irreps_ref.shape[1]
    first = first_ref[0]
    cd = tasks_ref[own]
    row = lambda pair, side: irreps_ref[pl.ds(pairs_ref[pair, side], 1), :]
    wide = lambda values: jnp.broadcast_to(values, (GROUP, tile))
    ab_outer, ab_inner = row(own, 0), row(own, 1)
    irrep = pair_rows(
        jnp.concatenate([wide(row(cd, 0)), wide(ab_outer)], axis=0),
        jnp.concatenate([wide(row(cd, 1)), wide(ab_inner)], axis=0),
        width,
    )
    cd_irrep, ab_irrep = irrep[:GROUP], irrep[GROUP:]
    rank = ranks(cd_irrep) - first
    inside = jnp.logical_and(rank >= 0, rank < depth)
    slot = jnp.where(inside, cd_irrep[:1] * depth + rank, -1)
    meta_ref[...] = jnp.where(iota((GROUP, width), 0) == 0, jnp.broadcast_to(slot, (GROUP, width)), ab_irrep)
    pair = iota((height, tile), 0) + block * height
    lane = iota((height, tile), 1)
    outer = jnp.sum(jnp.where(lane == lax.div(pair, tile), ab_outer, 0), axis=1, keepdims=True)
    inner = jnp.sum(jnp.where(lane == lax.rem(pair, tile), ab_inner, 0), axis=1, keepdims=True)
    live = jnp.bitwise_xor(outer, inner) == cd_irrep[:1]
    high, low = split(jnp.where(live, ints_ref[...], 0.0))
    pick = (iota((depth, width), 0) == rank).astype(jnp.bfloat16)
    both = dot(pick, jnp.concatenate([high, low], axis=0), NT)
    buf_ref[...] = both[:, :height] + both[:, height:]


def prep(first, tasks, pairs, irreps, ints, depth):
    height, width = ints.shape
    smem, vmem = pl.BlockSpec(memory_space=pltpu.SMEM), pl.BlockSpec(memory_space=pltpu.VMEM)
    return pl.pallas_call(
        functools.partial(prep_kernel, depth),
        out_shape=(
            jax.ShapeDtypeStruct((depth, height), jnp.float32),
            jax.ShapeDtypeStruct((GROUP, width), jnp.int32),
        ),
        in_specs=[smem, smem, smem, vmem, vmem],
        out_specs=(vmem, vmem),
        compiler_params=pltpu.CompilerParams(vmem_limit_bytes=32 << 20),
        cost_estimate=pl.CostEstimate(flops=4 * depth * height * width, bytes_accessed=4 * height * width, transcendentals=0),
        name="compact",
    )(first, tasks, pairs, irreps, ints)


def count_kernel(width, tasks_ref, pairs_ref, irreps_ref, most_ref):
    rows = lambda side: jnp.concatenate(
        [irreps_ref[pl.ds(pairs_ref[tasks_ref[k], side], 1), :] for k in range(tasks_ref.shape[0])], axis=0
    )
    irrep = pair_rows(rows(0), rows(1), width)
    most = jnp.zeros((irrep.shape[0], 1), jnp.int32)
    for g in range(GROUP):
        most = jnp.maximum(most, jnp.sum((irrep == g).astype(jnp.int32), axis=1, keepdims=True))
    most_ref[0] = jnp.max(most)


def count(tasks, pairs, irreps, width):
    smem, vmem = pl.BlockSpec(memory_space=pltpu.SMEM), pl.BlockSpec(memory_space=pltpu.VMEM)
    return pl.pallas_call(
        functools.partial(count_kernel, width),
        out_shape=jax.ShapeDtypeStruct((1,), jnp.int32),
        in_specs=[smem, smem, vmem],
        out_specs=smem,
        name="count",
    )(tasks, pairs, irreps)


def order_kernel(depth, count, *refs):
    tasks_ref, meta_ref = refs[:2]
    tiles, (out_ref, held, sem) = refs[2 : 2 + count], refs[2 + count :]
    own = lax.axis_index("vir")
    chosen = jnp.bitwise_xor(tasks_ref[own], own)
    copies = [pltpu.make_async_copy(tile_ref.at[:, 0, :], held, sem) for tile_ref in tiles]
    for number, copy in enumerate(copies):
        pl.when(chosen == number)(copy.start)
    width, slots, size = meta_ref.shape[1], GROUP * depth, 3 * LANES
    starts = range(0, slots, size)
    places = [(iota((min(size, slots - at), width), 0) + at == meta_ref[:1]).astype(jnp.bfloat16) for at in starts]
    copies[0].wait()
    both = jnp.concatenate(split(held[...]), axis=0)
    for at, place in zip(starts, places):
        out_ref[:, at : at + place.shape[0]] = dot(both, place, NT).astype(jnp.bfloat16)


def order(tasks, meta, tiles, depth):
    height, _, width = tiles[0].shape
    smem, vmem = pl.BlockSpec(memory_space=pltpu.SMEM), pl.BlockSpec(memory_space=pltpu.VMEM)
    return pl.pallas_call(
        functools.partial(order_kernel, depth, len(tiles)),
        out_shape=jax.ShapeDtypeStruct((2 * height, GROUP * depth), jnp.bfloat16),
        in_specs=[smem, vmem] + [pl.BlockSpec(memory_space=pltpu.HBM)] * len(tiles),
        out_specs=vmem,
        scratch_shapes=[pltpu.VMEM((height, width), jnp.float32), pltpu.SemaphoreType.DMA],
        compiler_params=pltpu.CompilerParams(vmem_limit_bytes=32 << 20),
        cost_estimate=pl.CostEstimate(
            flops=40 * height * width * GROUP * depth, bytes_accessed=4 * height * width, transcendentals=0
        ),
        name="order_amplitudes",
    )(tasks, meta, *tiles)


def ladder_kernel(depth, masks, count, meta_ref, amps_ref, *refs):
    pieces, (base_ref, out_ref, held, load_sem, store_sem) = refs[:count], refs[count:]
    block = lax.axis_index("occ")
    height, width = held.shape
    size = pieces[0].shape[1]
    pieces = [piece.at[at : at + depth] for piece in pieces for at in range(0, piece.shape[0], depth)]
    if size == width:
        places = [pl.ds(0, size)]
    else:
        places = [pl.ds(pl.multiple_of(jnp.bitwise_xor(block, mask) * size, LANES), size) for mask in masks]
    load = pltpu.make_async_copy(base_ref.at[:, 0, :], held, load_sem)
    load.start()
    high, low = split(jnp.concatenate([piece[...] for piece in pieces], axis=1))
    irrep = jnp.concatenate([meta_ref[1:2, place] for place in places], axis=1)
    zero = jnp.zeros((), jnp.bfloat16)
    blocks = lambda values: jnp.concatenate([jnp.where(irrep == g, values, zero) for g in range(GROUP)], axis=0)
    both = dot(amps_ref[...], blocks(high), NN)
    ladder = both[:height] + both[height:] + dot(amps_ref[:height], blocks(low), NN)
    load.wait()
    for n, place in enumerate(places):
        held[:, place] += ladder[:, n * size : (n + 1) * size]
    store = pltpu.make_async_copy(held, out_ref.at[:, 0, :], store_sem)
    store.start()
    store.wait()


def ladder(meta, amps, masks, pieces, base, depth):
    height, _, width = base.shape
    vmem, hbm = pl.BlockSpec(memory_space=pltpu.VMEM), pl.BlockSpec(memory_space=pl.ANY)
    return pl.pallas_call(
        functools.partial(ladder_kernel, depth, masks, len(pieces)),
        out_shape=jax.ShapeDtypeStruct(base.shape, base.dtype),
        in_specs=[vmem, vmem] + [vmem] * len(pieces) + [hbm],
        out_specs=hbm,
        scratch_shapes=[pltpu.VMEM((height, width), jnp.float32), pltpu.SemaphoreType.DMA, pltpu.SemaphoreType.DMA],
        compiler_params=pltpu.CompilerParams(vmem_limit_bytes=48 << 20),
        cost_estimate=pl.CostEstimate(
            flops=6 * height * width * GROUP * depth, bytes_accessed=8 * height * width, transcendentals=0
        ),
        name="ladder",
    )(meta, amps, *pieces, base)


def swap(values, axis, size, mask):
    return lax.ppermute(values, axis, [(device, device ^ mask) for device in range(size)])


def first_swaps(amps, size):
    return {0: amps, size >> 1: swap(amps, "vir", size, size >> 1)}


def other_swaps(tiles, size):
    bit = size >> 2
    while bit:
        for number in sorted(tiles):
            tiles[number | bit] = swap(tiles[number], "vir", size, bit)
        bit >>= 1
    return [tiles[number] for number in range(size)]


def after(value, earlier):
    return lax.optimization_barrier((value, earlier))[0]


def exchange(buf, size):
    lead = size >> 1
    even = [lead] + [mask for mask in range(2, size, 2) if mask != lead] if size > 2 else []
    near = {0: buf}
    for mask in even:
        near[mask] = swap(buf, "occ", size, mask) if mask <= lead else swap(near[mask & (mask - 1)], "occ", size, mask & -mask)
    blocks = {(mask,): piece for mask, piece in near.items()}
    groups = [(0,), tuple(even[-2::-1]), tuple(even[-1:])] if size > 1 else []
    for group in groups:
        if group:
            whole = jnp.concatenate([near[mask] for mask in group], axis=0) if len(group) > 1 else near[group[0]]
            blocks[tuple(mask | 1 for mask in group)] = swap(whole, "occ", size, 1)
    return blocks, [piece for masks, piece in blocks.items() if len(masks) == 1 and masks[0] <= lead]


def shards(occ_size, vir_size, amps, resid, ints, tasks, pair_tiles, irreps):
    rows = ints[0]
    height, width = rows.shape
    depth = min(DEPTH, width)

    def add_round(first, base):
        tiles = first_swaps(amps, vir_size)
        buf, meta = prep(first, tasks, pair_tiles, irreps, rows, depth)
        if height % LANES or occ_size & (occ_size - 1):
            blocks = {(0,): lax.all_gather(buf, "occ", axis=1, tiled=True)}
            tiles = other_swaps(tiles, vir_size)
        else:
            blocks, direct = exchange(buf, occ_size)
            tiles = {number: after(tile, direct) if number else tile for number, tile in tiles.items()}
            tiles = other_swaps(tiles, vir_size)
        tiles, base = lax.optimization_barrier((tiles, base))
        ordered = order(tasks, meta, tiles, depth)
        return ladder(meta, ordered, sum(blocks, ()), list(blocks.values()), base, depth)

    most = count(tasks, pair_tiles, irreps, width)
    rest = lax.while_loop(
        lambda state: state[0][0] < most[0],
        lambda state: (state[0] + depth, add_round(*state)),
        (jnp.full((1,), depth, jnp.int32), resid),
    )[1]
    return add_round(jnp.zeros((1,), jnp.int32), rest)


def solution(mesh):
    in_specs = (P("occ", "vir", None), P("occ", "vir", None), P("vir", "occ", None), P(), P(), P())
    out_specs = P("occ", "vir", None)
    body = functools.partial(shards, mesh.shape["occ"], mesh.shape["vir"])
    return jax.shard_map(body, mesh=mesh, in_specs=in_specs, out_specs=out_specs, check_vma=False)
```

```python
import functools

import jax
import jax.numpy as jnp
from jax import lax
from jax.experimental import pallas as pl
from jax.experimental.pallas import tpu as pltpu
from jax.sharding import PartitionSpec as P

GROUP = 8
LANES = 128
DEPTH = 176

NT = (((1,), (1,)), ((), ()))
NN = (((1,), (0,)), ((), ()))


def dot(left, right, dims):
    return lax.dot_general(left, right, dims, preferred_element_type=jnp.float32)


def split(values):
    high = values.astype(jnp.bfloat16)
    return high, (values - high.astype(jnp.float32)).astype(jnp.bfloat16)


def iota(shape, dim):
    return lax.broadcasted_iota(jnp.int32, shape, dim)


def pair_rows(firsts, seconds, width):
    tile = firsts.shape[1]
    column, orbital = iota((tile, width), 1), iota((tile, width), 0)
    outer = (lax.div(column, tile) == orbital).astype(jnp.bfloat16)
    inner = (lax.rem(column, tile) == orbital).astype(jnp.bfloat16)
    spread = lambda rows, how: dot(rows.astype(jnp.float32).astype(jnp.bfloat16), how, NN).astype(jnp.int32)
    return jnp.bitwise_xor(spread(firsts, outer), spread(seconds, inner))


def ranks(irrep):
    width = irrep.shape[1]
    member = (irrep == iota(irrep.shape, 0)).astype(jnp.float32)
    parts = [member[:, at : at + LANES] for at in range(0, width, LANES)]
    before = (iota((LANES, LANES), 0) < iota((LANES, LANES), 1)).astype(jnp.bfloat16)
    inside = dot(jnp.concatenate(parts, axis=0).astype(jnp.bfloat16), before, NN)
    base = jnp.zeros((GROUP, 1), jnp.float32)
    out = []
    for place, part in enumerate(parts):
        count = inside[place * GROUP : (place + 1) * GROUP] + base
        out.append(jnp.sum(part * count, axis=0, keepdims=True))
        base = base + jnp.sum(part, axis=1, keepdims=True)
    return jnp.concatenate(out, axis=1).astype(jnp.int32)


def prep_kernel(depth, first_ref, tasks_ref, pairs_ref, irreps_ref, ints_ref, buf_ref, meta_ref):
    own, block = lax.axis_index("vir"), lax.axis_index("occ")
    height, width = ints_ref.shape
    tile = irreps_ref.shape[1]
    first = first_ref[0]
    cd = tasks_ref[own]
    row = lambda pair, side: irreps_ref[pl.ds(pairs_ref[pair, side], 1), :]
    wide = lambda values: jnp.broadcast_to(values, (GROUP, tile))
    ab_outer, ab_inner = row(own, 0), row(own, 1)
    irrep = pair_rows(
        jnp.concatenate([wide(row(cd, 0)), wide(ab_outer)], axis=0),
        jnp.concatenate([wide(row(cd, 1)), wide(ab_inner)], axis=0),
        width,
    )
    cd_irrep, ab_irrep = irrep[:GROUP], irrep[GROUP:]
    rank = ranks(cd_irrep) - first
    inside = jnp.logical_and(rank >= 0, rank < depth)
    slot = jnp.where(inside, cd_irrep[:1] * depth + rank, -1)
    meta_ref[...] = jnp.where(iota((GROUP, width), 0) == 0, jnp.broadcast_to(slot, (GROUP, width)), ab_irrep)
    pair = iota((height, tile), 0) + block * height
    lane = iota((height, tile), 1)
    outer = jnp.sum(jnp.where(lane == lax.div(pair, tile), ab_outer, 0), axis=1, keepdims=True)
    inner = jnp.sum(jnp.where(lane == lax.rem(pair, tile), ab_inner, 0), axis=1, keepdims=True)
    live = jnp.bitwise_xor(outer, inner) == cd_irrep[:1]
    high, low = split(jnp.where(live, ints_ref[...], 0.0))
    pick = (iota((depth, width), 0) == rank).astype(jnp.bfloat16)
    buf_ref[...] = dot(pick, high, NT) + dot(pick, low, NT)


def prep(first, tasks, pairs, irreps, ints, depth):
    height, width = ints.shape
    smem, vmem = pl.BlockSpec(memory_space=pltpu.SMEM), pl.BlockSpec(memory_space=pltpu.VMEM)
    return pl.pallas_call(
        functools.partial(prep_kernel, depth),
        out_shape=(
            jax.ShapeDtypeStruct((depth, height), jnp.float32),
            jax.ShapeDtypeStruct((GROUP, width), jnp.int32),
        ),
        in_specs=[smem, smem, smem, vmem, vmem],
        out_specs=(vmem, vmem),
        compiler_params=pltpu.CompilerParams(vmem_limit_bytes=32 << 20),
        cost_estimate=pl.CostEstimate(flops=4 * depth * height * width, bytes_accessed=4 * height * width, transcendentals=0),
        name="compact",
    )(first, tasks, pairs, irreps, ints)


def count_kernel(width, tasks_ref, pairs_ref, irreps_ref, most_ref):
    rows = lambda side: jnp.concatenate(
        [irreps_ref[pl.ds(pairs_ref[tasks_ref[k], side], 1), :] for k in range(tasks_ref.shape[0])], axis=0
    )
    irrep = pair_rows(rows(0), rows(1), width)
    most = jnp.zeros((irrep.shape[0], 1), jnp.int32)
    for g in range(GROUP):
        most = jnp.maximum(most, jnp.sum((irrep == g).astype(jnp.int32), axis=1, keepdims=True))
    most_ref[0] = jnp.max(most)


def count(tasks, pairs, irreps, width):
    smem, vmem = pl.BlockSpec(memory_space=pltpu.SMEM), pl.BlockSpec(memory_space=pltpu.VMEM)
    return pl.pallas_call(
        functools.partial(count_kernel, width),
        out_shape=jax.ShapeDtypeStruct((1,), jnp.int32),
        in_specs=[smem, smem, vmem],
        out_specs=smem,
        name="count",
    )(tasks, pairs, irreps)


def order_kernel(depth, count, *refs):
    tasks_ref, meta_ref = refs[:2]
    tiles, (base_ref, out_ref, rows_ref, held, sem, base_sem) = refs[2 : 2 + count], refs[2 + count :]
    own = lax.axis_index("vir")
    chosen = jnp.bitwise_xor(tasks_ref[own], own)
    copies = [pltpu.make_async_copy(tile_ref.at[:, 0, :], held, sem) for tile_ref in tiles]
    for number, copy in enumerate(copies):
        pl.when(chosen == number)(copy.start)
    load = pltpu.make_async_copy(base_ref.at[:, 0, :], rows_ref, base_sem)
    load.start()
    width, slots, size = meta_ref.shape[1], GROUP * depth, 3 * LANES
    starts = range(0, slots, size)
    places = [(iota((min(size, slots - at), width), 0) + at == meta_ref[:1]).astype(jnp.bfloat16) for at in starts]
    copies[0].wait()
    both = jnp.concatenate(split(held[...]), axis=0)
    for at, place in zip(starts, places):
        out_ref[:, at : at + place.shape[0]] = dot(both, place, NT).astype(jnp.bfloat16)
    load.wait()


def order(tasks, meta, tiles, base, depth):
    height, _, width = tiles[0].shape
    smem, vmem = pl.BlockSpec(memory_space=pltpu.SMEM), pl.BlockSpec(memory_space=pltpu.VMEM)
    return pl.pallas_call(
        functools.partial(order_kernel, depth, len(tiles)),
        out_shape=(
            jax.ShapeDtypeStruct((2 * height, GROUP * depth), jnp.bfloat16),
            jax.ShapeDtypeStruct((height, width), base.dtype),
        ),
        in_specs=[smem, vmem] + [pl.BlockSpec(memory_space=pltpu.HBM)] * len(tiles) + [pl.BlockSpec(memory_space=pl.ANY)],
        out_specs=(vmem, vmem),
        scratch_shapes=[pltpu.VMEM((height, width), jnp.float32), pltpu.SemaphoreType.DMA, pltpu.SemaphoreType.DMA],
        compiler_params=pltpu.CompilerParams(vmem_limit_bytes=32 << 20),
        cost_estimate=pl.CostEstimate(
            flops=40 * height * width * GROUP * depth, bytes_accessed=4 * height * width, transcendentals=0
        ),
        name="order_amplitudes",
    )(tasks, meta, *tiles, base)


def ladder_kernel(depth, masks, count, meta_ref, amps_ref, *refs):
    pieces, (base_ref, out_ref, held, store_sem) = refs[:count], refs[count:]
    block = lax.axis_index("occ")
    height, width = held.shape
    size = pieces[0].shape[1]
    pieces = [piece.at[at : at + depth] for piece in pieces for at in range(0, piece.shape[0], depth)]
    if size == width:
        places = [pl.ds(0, size)]
    else:
        places = [pl.ds(pl.multiple_of(jnp.bitwise_xor(block, mask) * size, LANES), size) for mask in masks]
    high, low = split(jnp.concatenate([piece[...] for piece in pieces], axis=1))
    irrep = jnp.concatenate([meta_ref[1:2, place] for place in places], axis=1)
    zero = jnp.zeros((), jnp.bfloat16)
    blocks = lambda values: jnp.concatenate([jnp.where(irrep == g, values, zero) for g in range(GROUP)], axis=0)
    both = dot(amps_ref[...], blocks(high), NN)
    ladder = both[:height] + both[height:] + dot(amps_ref[:height], blocks(low), NN)
    for n, place in enumerate(places):
        held[:, place] = base_ref[:, place] + ladder[:, n * size : (n + 1) * size]
    store = pltpu.make_async_copy(held, out_ref.at[:, 0, :], store_sem)
    store.start()
    store.wait()


def ladder(meta, amps, masks, pieces, base, depth):
    height, width = base.shape
    vmem, hbm = pl.BlockSpec(memory_space=pltpu.VMEM), pl.BlockSpec(memory_space=pl.ANY)
    return pl.pallas_call(
        functools.partial(ladder_kernel, depth, masks, len(pieces)),
        out_shape=jax.ShapeDtypeStruct((height, 1, width), base.dtype),
        in_specs=[vmem, vmem] + [vmem] * len(pieces) + [vmem],
        out_specs=hbm,
        scratch_shapes=[pltpu.VMEM((height, width), jnp.float32), pltpu.SemaphoreType.DMA],
        compiler_params=pltpu.CompilerParams(vmem_limit_bytes=48 << 20),
        cost_estimate=pl.CostEstimate(
            flops=6 * height * width * GROUP * depth, bytes_accessed=8 * height * width, transcendentals=0
        ),
        name="ladder",
    )(meta, amps, *pieces, base)


def swap(values, axis, size, mask):
    return lax.ppermute(values, axis, [(device, device ^ mask) for device in range(size)])


def first_swaps(amps, size):
    return {0: amps, size >> 1: swap(amps, "vir", size, size >> 1)}


def other_swaps(tiles, size):
    bit = size >> 2
    while bit:
        for number in sorted(tiles):
            tiles[number | bit] = swap(tiles[number], "vir", size, bit)
        bit >>= 1
    return [tiles[number] for number in range(size)]


def after(value, earlier):
    return lax.optimization_barrier((value, earlier))[0]


def exchange(buf, size):
    lead = size >> 1
    even = [lead] + [mask for mask in range(2, size, 2) if mask != lead] if size > 2 else []
    near = {0: buf}
    for mask in even:
        near[mask] = swap(buf, "occ", size, mask) if mask <= lead else swap(near[mask & (mask - 1)], "occ", size, mask & -mask)
    blocks = {(mask,): piece for mask, piece in near.items()}
    groups = [(0,), tuple(even[-2::-1]), tuple(even[-1:])] if size > 1 else []
    for group in groups:
        if group:
            whole = jnp.concatenate([near[mask] for mask in group], axis=0) if len(group) > 1 else near[group[0]]
            blocks[tuple(mask | 1 for mask in group)] = swap(whole, "occ", size, 1)
    return blocks, [piece for masks, piece in blocks.items() if len(masks) == 1 and masks[0] <= lead]


def shards(occ_size, vir_size, amps, resid, ints, tasks, pair_tiles, irreps):
    rows = ints[0]
    height, width = rows.shape
    depth = min(DEPTH, width)

    def add_round(first, base):
        tiles = first_swaps(amps, vir_size)
        buf, meta = prep(first, tasks, pair_tiles, irreps, rows, depth)
        if height % LANES or occ_size & (occ_size - 1):
            blocks = {(0,): lax.all_gather(buf, "occ", axis=1, tiled=True)}
            tiles = other_swaps(tiles, vir_size)
        else:
            blocks, direct = exchange(buf, occ_size)
            tiles = {number: after(tile, direct) if number else tile for number, tile in tiles.items()}
            tiles = other_swaps(tiles, vir_size)
        tiles, base = lax.optimization_barrier((tiles, base))
        ordered, base = order(tasks, meta, tiles, base, depth)
        return ladder(meta, ordered, sum(blocks, ()), list(blocks.values()), base, depth)

    most = count(tasks, pair_tiles, irreps, width)
    rest = lax.while_loop(
        lambda state: state[0][0] < most[0],
        lambda state: (state[0] + depth, add_round(*state)),
        (jnp.full((1,), depth, jnp.int32), resid),
    )[1]
    return add_round(jnp.zeros((1,), jnp.int32), rest)


def solution(mesh):
    in_specs = (P("occ", "vir", None), P("occ", "vir", None), P("vir", "occ", None), P(), P(), P())
    out_specs = P("occ", "vir", None)
    body = functools.partial(shards, mesh.shape["occ"], mesh.shape["vir"])
    return jax.shard_map(body, mesh=mesh, in_specs=in_specs, out_specs=out_specs, check_vma=False)
```

```python
import functools

import jax
import jax.numpy as jnp
from jax import lax
from jax.experimental import pallas as pl
from jax.experimental.pallas import tpu as pltpu
from jax.sharding import PartitionSpec as P

GROUP = 8
LANES = 128
DEPTH = 176

NT = (((1,), (1,)), ((), ()))
NN = (((1,), (0,)), ((), ()))


def dot(left, right, dims):
    return lax.dot_general(left, right, dims, preferred_element_type=jnp.float32)


def split(values):
    high = values.astype(jnp.bfloat16)
    return high, (values - high.astype(jnp.float32)).astype(jnp.bfloat16)


def iota(shape, dim):
    return lax.broadcasted_iota(jnp.int32, shape, dim)


def pair_rows(firsts, seconds, width):
    tile = firsts.shape[1]
    column, orbital = iota((tile, width), 1), iota((tile, width), 0)
    outer = (lax.div(column, tile) == orbital).astype(jnp.bfloat16)
    inner = (lax.rem(column, tile) == orbital).astype(jnp.bfloat16)
    spread = lambda rows, how: dot(rows.astype(jnp.float32).astype(jnp.bfloat16), how, NN).astype(jnp.int32)
    return jnp.bitwise_xor(spread(firsts, outer), spread(seconds, inner))


def ranks(irrep):
    width = irrep.shape[1]
    member = (irrep == iota(irrep.shape, 0)).astype(jnp.float32)
    parts = [member[:, at : at + LANES] for at in range(0, width, LANES)]
    before = (iota((LANES, LANES), 0) < iota((LANES, LANES), 1)).astype(jnp.bfloat16)
    inside = dot(jnp.concatenate(parts, axis=0).astype(jnp.bfloat16), before, NN)
    base = jnp.zeros((GROUP, 1), jnp.float32)
    out = []
    for place, part in enumerate(parts):
        count = inside[place * GROUP : (place + 1) * GROUP] + base
        out.append(jnp.sum(part * count, axis=0, keepdims=True))
        base = base + jnp.sum(part, axis=1, keepdims=True)
    return jnp.concatenate(out, axis=1).astype(jnp.int32)


def prep_kernel(depth, first_ref, tasks_ref, pairs_ref, irreps_ref, ints_ref, buf_ref, meta_ref):
    own, block = lax.axis_index("vir"), lax.axis_index("occ")
    height, width = ints_ref.shape
    tile = irreps_ref.shape[1]
    first = first_ref[0]
    cd = tasks_ref[own]
    row = lambda pair, side: irreps_ref[pl.ds(pairs_ref[pair, side], 1), :]
    wide = lambda values: jnp.broadcast_to(values, (GROUP, tile))
    ab_outer, ab_inner = row(own, 0), row(own, 1)
    irrep = pair_rows(
        jnp.concatenate([wide(row(cd, 0)), wide(ab_outer)], axis=0),
        jnp.concatenate([wide(row(cd, 1)), wide(ab_inner)], axis=0),
        width,
    )
    cd_irrep, ab_irrep = irrep[:GROUP], irrep[GROUP:]
    rank = ranks(cd_irrep) - first
    inside = jnp.logical_and(rank >= 0, rank < depth)
    slot = jnp.where(inside, cd_irrep[:1] * depth + rank, -1)
    meta_ref[...] = jnp.where(iota((GROUP, width), 0) == 0, jnp.broadcast_to(slot, (GROUP, width)), ab_irrep)
    pair = iota((height, tile), 0) + block * height
    lane = iota((height, tile), 1)
    outer = jnp.sum(jnp.where(lane == lax.div(pair, tile), ab_outer, 0), axis=1, keepdims=True)
    inner = jnp.sum(jnp.where(lane == lax.rem(pair, tile), ab_inner, 0), axis=1, keepdims=True)
    live = jnp.bitwise_xor(outer, inner) == cd_irrep[:1]
    high, low = split(jnp.where(live, ints_ref[...], 0.0))
    pick = (iota((depth, width), 0) == rank).astype(jnp.bfloat16)
    both = dot(pick, jnp.concatenate([high, low], axis=0), NT)
    buf_ref[...] = both[:, :height] + both[:, height:]


def prep(first, tasks, pairs, irreps, ints, depth):
    height, width = ints.shape
    smem, vmem = pl.BlockSpec(memory_space=pltpu.SMEM), pl.BlockSpec(memory_space=pltpu.VMEM)
    return pl.pallas_call(
        functools.partial(prep_kernel, depth),
        out_shape=(
            jax.ShapeDtypeStruct((depth, height), jnp.float32),
            jax.ShapeDtypeStruct((GROUP, width), jnp.int32),
        ),
        in_specs=[smem, smem, smem, vmem, vmem],
        out_specs=(vmem, vmem),
        compiler_params=pltpu.CompilerParams(vmem_limit_bytes=32 << 20),
        cost_estimate=pl.CostEstimate(flops=4 * depth * height * width, bytes_accessed=4 * height * width, transcendentals=0),
        name="compact",
    )(first, tasks, pairs, irreps, ints)


def count_kernel(width, tasks_ref, pairs_ref, irreps_ref, most_ref):
    rows = lambda side: jnp.concatenate(
        [irreps_ref[pl.ds(pairs_ref[tasks_ref[k], side], 1), :] for k in range(tasks_ref.shape[0])], axis=0
    )
    irrep = pair_rows(rows(0), rows(1), width)
    most = jnp.zeros((irrep.shape[0], 1), jnp.int32)
    for g in range(GROUP):
        most = jnp.maximum(most, jnp.sum((irrep == g).astype(jnp.int32), axis=1, keepdims=True))
    most_ref[0] = jnp.max(most)


def count(tasks, pairs, irreps, width):
    smem, vmem = pl.BlockSpec(memory_space=pltpu.SMEM), pl.BlockSpec(memory_space=pltpu.VMEM)
    return pl.pallas_call(
        functools.partial(count_kernel, width),
        out_shape=jax.ShapeDtypeStruct((1,), jnp.int32),
        in_specs=[smem, smem, vmem],
        out_specs=smem,
        name="count",
    )(tasks, pairs, irreps)


def order_kernel(depth, count, *refs):
    tasks_ref, meta_ref = refs[:2]
    tiles, (base_ref, out_ref, rows_ref, held, sem, base_sem) = refs[2 : 2 + count], refs[2 + count :]
    own = lax.axis_index("vir")
    chosen = jnp.bitwise_xor(tasks_ref[own], own)
    copies = [pltpu.make_async_copy(tile_ref.at[:, 0, :], held, sem) for tile_ref in tiles]
    for number, copy in enumerate(copies):
        pl.when(chosen == number)(copy.start)
    load = pltpu.make_async_copy(base_ref.at[:, 0, :], rows_ref, base_sem)
    load.start()
    width, slots, size = meta_ref.shape[1], GROUP * depth, 3 * LANES
    starts = range(0, slots, size)
    places = [(iota((min(size, slots - at), width), 0) + at == meta_ref[:1]).astype(jnp.bfloat16) for at in starts]
    copies[0].wait()
    both = jnp.concatenate(split(held[...]), axis=0)
    for at, place in zip(starts, places):
        out_ref[:, at : at + place.shape[0]] = dot(both, place, NT).astype(jnp.bfloat16)
    load.wait()


def order(tasks, meta, tiles, base, depth):
    height, _, width = tiles[0].shape
    smem, vmem = pl.BlockSpec(memory_space=pltpu.SMEM), pl.BlockSpec(memory_space=pltpu.VMEM)
    return pl.pallas_call(
        functools.partial(order_kernel, depth, len(tiles)),
        out_shape=(
            jax.ShapeDtypeStruct((2 * height, GROUP * depth), jnp.bfloat16),
            jax.ShapeDtypeStruct((height, width), base.dtype),
        ),
        in_specs=[smem, vmem] + [pl.BlockSpec(memory_space=pltpu.HBM)] * len(tiles) + [pl.BlockSpec(memory_space=pl.ANY)],
        out_specs=(vmem, vmem),
        scratch_shapes=[pltpu.VMEM((height, width), jnp.float32), pltpu.SemaphoreType.DMA, pltpu.SemaphoreType.DMA],
        compiler_params=pltpu.CompilerParams(vmem_limit_bytes=32 << 20),
        cost_estimate=pl.CostEstimate(
            flops=40 * height * width * GROUP * depth, bytes_accessed=4 * height * width, transcendentals=0
        ),
        name="order_amplitudes",
    )(tasks, meta, *tiles, base)


def ladder_kernel(depth, masks, count, meta_ref, amps_ref, *refs):
    pieces, (base_ref, out_ref, held, store_sem) = refs[:count], refs[count:]
    block = lax.axis_index("occ")
    height, width = held.shape
    size = pieces[0].shape[1]
    pieces = [piece.at[at : at + depth] for piece in pieces for at in range(0, piece.shape[0], depth)]
    if size == width:
        places = [pl.ds(0, size)]
    else:
        places = [pl.ds(pl.multiple_of(jnp.bitwise_xor(block, mask) * size, LANES), size) for mask in masks]
    high, low = split(jnp.concatenate([piece[...] for piece in pieces], axis=1))
    irrep = jnp.concatenate([meta_ref[1:2, place] for place in places], axis=1)
    zero = jnp.zeros((), jnp.bfloat16)
    blocks = lambda values: jnp.concatenate([jnp.where(irrep == g, values, zero) for g in range(GROUP)], axis=0)
    both = dot(amps_ref[...], blocks(high), NN)
    ladder = both[:height] + both[height:] + dot(amps_ref[:height], blocks(low), NN)
    for n, place in enumerate(places):
        held[:, place] = base_ref[:, place] + ladder[:, n * size : (n + 1) * size]
    store = pltpu.make_async_copy(held, out_ref.at[:, 0, :], store_sem)
    store.start()
    store.wait()


def ladder(meta, amps, masks, pieces, base, depth):
    height, width = base.shape
    vmem, hbm = pl.BlockSpec(memory_space=pltpu.VMEM), pl.BlockSpec(memory_space=pl.ANY)
    return pl.pallas_call(
        functools.partial(ladder_kernel, depth, masks, len(pieces)),
        out_shape=jax.ShapeDtypeStruct((height, 1, width), base.dtype),
        in_specs=[vmem, vmem] + [vmem] * len(pieces) + [vmem],
        out_specs=hbm,
        scratch_shapes=[pltpu.VMEM((height, width), jnp.float32), pltpu.SemaphoreType.DMA],
        compiler_params=pltpu.CompilerParams(vmem_limit_bytes=48 << 20),
        cost_estimate=pl.CostEstimate(
            flops=6 * height * width * GROUP * depth, bytes_accessed=8 * height * width, transcendentals=0
        ),
        name="ladder",
    )(meta, amps, *pieces, base)


def swap(values, axis, size, mask):
    return lax.ppermute(values, axis, [(device, device ^ mask) for device in range(size)])


def first_swaps(amps, size):
    return {0: amps, size >> 1: swap(amps, "vir", size, size >> 1)}


def other_swaps(tiles, size):
    bit = size >> 2
    while bit:
        for number in sorted(tiles):
            tiles[number | bit] = swap(tiles[number], "vir", size, bit)
        bit >>= 1
    return [tiles[number] for number in range(size)]


def after(value, earlier):
    return lax.optimization_barrier((value, earlier))[0]


def exchange(buf, size):
    lead = size >> 1
    even = [lead] + [mask for mask in range(2, size, 2) if mask != lead] if size > 2 else []
    near = {0: buf}
    for mask in even:
        near[mask] = swap(buf, "occ", size, mask) if mask <= lead else swap(near[mask & (mask - 1)], "occ", size, mask & -mask)
    blocks = {(mask,): piece for mask, piece in near.items()}
    groups = [(0,), tuple(even[-2::-1]), tuple(even[-1:])] if size > 1 else []
    for group in groups:
        if group:
            whole = jnp.concatenate([near[mask] for mask in group], axis=0) if len(group) > 1 else near[group[0]]
            blocks[tuple(mask | 1 for mask in group)] = swap(whole, "occ", size, 1)
    return blocks, [piece for masks, piece in blocks.items() if len(masks) == 1 and masks[0] <= lead]


def shards(occ_size, vir_size, amps, resid, ints, tasks, pair_tiles, irreps):
    rows = ints[0]
    height, width = rows.shape
    depth = min(DEPTH, width)

    def add_round(first, base):
        tiles = first_swaps(amps, vir_size)
        buf, meta = prep(first, tasks, pair_tiles, irreps, rows, depth)
        if height % LANES or occ_size & (occ_size - 1):
            blocks = {(0,): lax.all_gather(buf, "occ", axis=1, tiled=True)}
            tiles = other_swaps(tiles, vir_size)
        else:
            blocks, direct = exchange(buf, occ_size)
            tiles = {number: after(tile, direct) if number else tile for number, tile in tiles.items()}
            tiles = other_swaps(tiles, vir_size)
        tiles, base = lax.optimization_barrier((tiles, base))
        ordered, base = order(tasks, meta, tiles, base, depth)
        return ladder(meta, ordered, sum(blocks, ()), list(blocks.values()), base, depth)

    most = count(tasks, pair_tiles, irreps, width)
    rest = lax.while_loop(
        lambda state: state[0][0] < most[0],
        lambda state: (state[0] + depth, add_round(*state)),
        (jnp.full((1,), depth, jnp.int32), resid),
    )[1]
    return add_round(jnp.zeros((1,), jnp.int32), rest)


def solution(mesh):
    in_specs = (P("occ", "vir", None), P("occ", "vir", None), P("vir", "occ", None), P(), P(), P())
    out_specs = P("occ", "vir", None)
    body = functools.partial(shards, mesh.shape["occ"], mesh.shape["vir"])
    return jax.shard_map(body, mesh=mesh, in_specs=in_specs, out_specs=out_specs, check_vma=False)
```
